256 devices in a mesh: dp: 8 (over z_hi, x), ctx: 32 (over y, z_lo, core).
Axes of the slice: x: 4, y: 4, z: 8 (z_hi: 2, z_lo: 4; z = z_hi * 4 + z_lo), core: 2. Of those that a mesh axis runs over, the one named last changes fastest.
Arguments:
- inputs: bfloat16 [256, 512, 1536], P('ctx', 'dp'), may hold values from -6 to 6
- cotangent: bfloat16 [256, 512, 1536], P('ctx', 'dp'), may hold values from -6 to 6
- w_in: bfloat16 [1536, 1536], P('dp'), may hold values from -0.15625 to 0.15625
- factor_one: bfloat16 [512, 512], replicated, may hold values from -0.25 to 0.25
- factor_two: bfloat16 [256, 256], replicated, may hold values from -0.375 to 0.375
- kernel: float32 [256, 512], P('ctx'), may hold values from 0.3 to 3
Outputs:
- grad_inputs: bfloat16 [256, 512, 1536], P('ctx', 'dp')
- grad_w_in: float32 [1536, 1536], P('dp')
- grad_one: float32 [512, 512], replicated
- grad_two: float32 [256, 256], replicated
- grad_kernel: float32 [256, 512], P('ctx')
The draws below stay inside these ranges and needn't reach their ends.
All inputs are finite; a program needn't handle non-finite values.
Results may differ from the reference program's by a relative error of at most 0.0067.
Values may be sent and summed in bfloat16 or wider, within the bound.
No kernel may reach another device: no remote copies, remote signals or barrier semaphores. Data moves between devices by JAX's collectives and lax.ppermute only.
A program may use at most 128 MiB of HBM per device.

```python
import math
import jax
import jax.numpy as jnp
from jax import lax

D = 1536
BLK = 512
BLOCKS = 256
SEQ = 131072


def strengthened(drawn, stream_key, source, target, blocks, factor):
    owner, partner = [(jnp.arange(drawn.shape[position]) // (drawn.shape[position] // blocks)).reshape([-1 if axis == position else 1 for axis in range(drawn.ndim)]) for position in (source, target)]
    chosen = jax.random.permutation(stream_key, blocks)[partner]
    strong = (owner == chosen) | (owner == (partner + blocks // 2) % blocks)
    return jnp.where(strong, factor * drawn, drawn)


def block_scale(rng, dims, shards, smallest, high):
    def one(dim, parts):
        draws = jax.random.uniform(jax.random.fold_in(jax.random.fold_in(rng, 6), dim), (parts,), jnp.float32, smallest / len(shards), high / len(shards))
        return jnp.repeat(jnp.exp(draws), dims[dim] // parts).reshape((-1,) + (1,) * (len(dims) - dim - 1))

    gain = one(*shards[0])
    for cut in shards[1:]:
        gain = gain * one(*cut)
    return gain


def gaussian(rng, extent, deviation, limit, split=(), held_as=jnp.bfloat16):
    array = jax.random.normal(rng, extent, jnp.float32) * deviation
    if len(split) > 0:
        array = block_scale(rng, extent, split, -0.22, 0.18) * array
    return jnp.clip(array, min=-limit, max=limit).astype(held_as)


def bell_draw_with(key, dims, spread, limit, pieces, heavy, kind=jnp.bfloat16):
    drawn = spread * jax.random.normal(key, dims, jnp.float32)
    if pieces:
        drawn = drawn * block_scale(key, dims, pieces, -0.22, 0.18)
    return jnp.clip(strengthened(drawn, jax.random.fold_in(key, 3), *heavy), -limit, limit).astype(kind)


def setup_inputs(seed: int = 0) -> dict:
    streams_of = jax.random.split(jax.random.key(seed), 7)
    return {
        "inputs": bell_draw_with(streams_of[0], (BLOCKS, BLK, D), 1.0, 6.0, ((0, 32), (1, 8)), (0, 2, 32, 2.75)),
        "cotangent": gaussian(streams_of[1], (BLOCKS, BLK, D), 1.0, 6.0, ((0, 32), (1, 8))),
        "w_in": gaussian(streams_of[2], (D, D), D ** -0.5, 0.15625, ((0, 8),)),
        "factor_one": gaussian(streams_of[3], (BLK, BLK), BLK ** -0.5, 0.25),
        "factor_two": gaussian(streams_of[4], (BLOCKS, BLOCKS), BLOCKS ** -0.5, 0.375),
        "kernel": jnp.clip(jnp.exp(math.log(3.0) - 2.3025851 * jax.random.uniform(streams_of[5], (BLOCKS, BLK), jnp.float32) ** block_scale(streams_of[5], (BLOCKS, BLK), ((0, 32),), -0.2, 0.2)), 0.3, 3.0),
    }


def reference(inputs, cotangent, w_in, factor_one, factor_two, kernel):
    f32 = jnp.float32
    bf16 = jnp.bfloat16
    rows_in = inputs.reshape(SEQ, D)
    projected = jnp.dot(rows_in, w_in, preferred_element_type=f32).astype(bf16).reshape(BLOCKS, BLK, D)
    grad_mixed = (cotangent.astype(f32) * inputs.astype(f32)).astype(bf16)
    group = 128 if D % 128 == 0 else D
    groups = D // group
    one_f = factor_one.astype(f32)
    two_f = factor_two.astype(f32)

    def channel_group(carry, index):
        one_acc, two_acc, kernel_acc = carry
        start = (index * group).astype(jnp.int32)
        proj_g = lax.dynamic_slice_in_dim(projected, start, group, 2).astype(f32)
        grad_g = lax.dynamic_slice_in_dim(grad_mixed, start, group, 2).astype(f32)
        inner = jnp.einsum('pq,aqc->apc', one_f, proj_g)
        scaled = (kernel[:, :, None] * inner).astype(bf16)
        mixed = jnp.einsum('ij,jbc->ibc', two_f, scaled.astype(f32)).astype(bf16)
        grad_scaled = jnp.einsum('ij,ibc->jbc', two_f, grad_g).astype(bf16)
        two_acc = two_acc + jnp.einsum('ibc,jbc->ij', grad_g, scaled.astype(f32))
        kernel_acc = kernel_acc + lax.optimization_barrier(jnp.sum(grad_scaled.astype(f32) * inner, axis=2))
        grad_inner = (kernel[:, :, None] * grad_scaled.astype(f32)).astype(bf16)
        one_acc = one_acc + jnp.einsum('apc,aqc->pq', grad_inner.astype(f32), proj_g)
        grad_proj = jnp.einsum('pq,apc->aqc', one_f, grad_inner.astype(f32)).astype(bf16)
        return ((one_acc, two_acc, kernel_acc), (grad_proj, mixed))
    start_carry = (jnp.zeros((BLK, BLK), f32), jnp.zeros((BLOCKS, BLOCKS), f32), jnp.zeros((BLOCKS, BLK), f32))
    final, stacked = lax.scan(channel_group, start_carry, jnp.arange(groups, dtype=jnp.int32))
    one_acc, two_acc, kernel_acc = final
    grad_proj = jnp.moveaxis(stacked[0], 0, 2).reshape(SEQ, D)
    mixed = jnp.moveaxis(stacked[1], 0, 2).reshape(SEQ, D)
    win_sum = jnp.dot(rows_in.T, grad_proj, preferred_element_type=f32)
    back = jnp.dot(grad_proj, w_in.T, preferred_element_type=f32)
    cot_rows = cotangent.reshape(SEQ, D)
    grad_inputs = (back + cot_rows.astype(f32) * mixed.astype(f32)).astype(bf16).reshape(BLOCKS, BLK, D)
    grad_w_in = win_sum / jnp.sqrt(jnp.float32(SEQ))
    grad_one = one_acc / jnp.sqrt(jnp.float32(BLOCKS * D))
    grad_two = two_acc / jnp.sqrt(jnp.float32(BLK * D))
    grad_kernel = kernel_acc / jnp.sqrt(jnp.float32(D))
    return (grad_inputs, grad_w_in, grad_one, grad_two, grad_kernel)
```

```python
import math

import jax
import jax.numpy as jnp
from jax import lax
from jax.sharding import Mesh
from jax.sharding import PartitionSpec as P

F32 = jnp.float32
BF16 = jnp.bfloat16
ALL = ("zh", "x", "y", "zl", "c")
DP = ("zh", "x")
CTX = ("y", "zl", "c")


def exchange(array, axes):
    return lax.all_to_all(array, axes, 0, 0, tiled=True)


def gather_w(w_in):
    rows, width = w_in.shape
    piece = rows // 8
    place = lax.axis_index("y") * 2 + lax.axis_index("c")
    mine = lax.dynamic_slice_in_dim(w_in, place * piece, piece, 0)
    other = lax.ppermute(mine, "zh", [(0, 1), (1, 0)])
    low = lax.axis_index("zh") == 0
    both = jnp.concatenate([jnp.where(low, mine, other), jnp.where(low, other, mine)], 0)
    whole = lax.all_gather(both, ("x", "y", "c"), axis=0, tiled=True)
    whole = whole.reshape(4, 8, 2, piece, width).transpose(2, 0, 1, 3, 4)
    return whole.reshape(8 * rows, width)


def per_device(inputs, cotangent, w_in, factor_one, factor_two, kernel):
    blocks, pos, width = inputs.shape
    tokens = blocks * pos
    devices = 256
    chans = width // devices
    block_len = factor_one.shape[0]
    block_count = factor_two.shape[0]

    def to_channels(array_t):
        send = array_t.reshape(chans, devices, tokens).transpose(1, 0, 2)
        got = exchange(send.reshape(devices, -1, 128), ALL)
        got = got.reshape(8, 32, chans, blocks, pos).transpose(2, 1, 3, 0, 4)
        return got.reshape(chans, block_count, block_len)

    def to_home(array):
        send = array.reshape(chans, 32, blocks, 8, pos).transpose(3, 1, 0, 2, 4)
        got = exchange(send.reshape(devices, -1, 128), ALL)
        got = got.reshape(devices, chans, tokens).transpose(1, 0, 2)
        return got.reshape(width, tokens)

    rows_in = inputs.reshape(tokens, width)
    cot_rows = cotangent.reshape(tokens, width)
    xc = to_channels(rows_in.T)
    whole_w = gather_w(w_in)
    scale = lax.all_gather(kernel, CTX, axis=0, tiled=True)
    grad_mixed = (cot_rows.astype(F32) * rows_in.astype(F32)).astype(BF16)
    yc = jnp.einsum("jaq,pq->jap", xc, factor_one, preferred_element_type=F32)
    sc = (scale[None] * yc).astype(BF16)
    mc = jnp.einsum("il,jlp->jip", factor_two, sc, preferred_element_type=F32).astype(BF16)
    mixed_t = to_home(mc)
    ht = lax.dot_general(
        whole_w, grad_mixed, (((1,), (1,)), ((), ())), preferred_element_type=F32
    ).astype(BF16)
    hc = to_channels(ht)
    uc = jnp.einsum("il,jip->jlp", factor_two, hc, preferred_element_type=F32)
    kernel_term = jnp.sum(uc * yc, axis=0)
    tc = (scale[None] * uc).astype(BF16)
    back_c = jnp.einsum("jap,pq->jaq", tc, factor_one, preferred_element_type=F32).astype(BF16)
    back_t = to_home(back_c)
    one_term = jnp.einsum("jap,jaq->pq", tc, xc, preferred_element_type=F32)
    two_term = jnp.einsum("jip,jlp->il", hc, sc, preferred_element_type=F32)
    win_term = jnp.dot(mixed_t, grad_mixed, preferred_element_type=F32)

    extra = jnp.concatenate(
        [
            one_term.reshape(devices, -1),
            two_term.reshape(devices, -1),
            kernel_term.reshape(32, blocks, 8, pos).transpose(2, 0, 1, 3).reshape(devices, -1),
        ],
        1,
    ).astype(BF16)
    pieces = jnp.concatenate([win_term.astype(BF16).reshape(devices, -1), extra], 1)
    lines = pieces.shape[1] // 128
    pieces = pieces.reshape(2, 4, 4, 4, 2, lines, 128).transpose(4, 0, 1, 2, 3, 5, 6)
    got = exchange(pieces.reshape(-1, 128), ("c",)).reshape(2, -1, 128)
    part = (got[0].astype(F32) + got[1].astype(F32)).astype(BF16)
    part = part.reshape(2, 16, 4, lines, 128).transpose(1, 0, 2, 3, 4)
    got = exchange(part.reshape(-1, 128), ("x", "y")).reshape(16, -1, 128)
    part = jnp.sum(got.astype(F32), 0).astype(BF16)
    got = exchange(part, ("zh", "zl")).reshape(8, lines, 128)
    part = jnp.sum(got.astype(F32), 0)

    win_lines = width * width // devices // 128
    small = part[win_lines:].astype(BF16)
    small = exchange(jnp.broadcast_to(small[None], (8,) + small.shape), DP)
    one_two = small[:, :10]
    mine = jnp.concatenate([part[:win_lines].astype(BF16), one_two.reshape(-1, 128)], 0)
    got = exchange(jnp.broadcast_to(mine[None], (32,) + mine.shape), CTX)
    win_total = got[:, :win_lines].astype(F32).reshape(width // 8, width)
    one_two = got[:, win_lines:].reshape(32, 8, 10, 128).transpose(1, 0, 2, 3)
    one_total = one_two[:, :, :8].astype(F32).reshape(block_len, block_len)
    two_total = one_two[:, :, 8:].astype(F32).reshape(block_count, block_count)
    kernel_total = small[:, 10:].astype(F32).reshape(8, blocks, pos).transpose(1, 0, 2)
    grad_kernel = kernel_total.reshape(blocks, block_len) / math.sqrt(width)
    grad_one = one_total / math.sqrt(block_count * width)
    grad_two = two_total / math.sqrt(block_len * width)
    grad_w_in = win_total / math.sqrt(block_count * block_len)

    mixed = lax.dot_general(
        mixed_t, whole_w, (((0,), (0,)), ((), ())), preferred_element_type=F32
    ).astype(BF16)
    grad_in = back_t.T.astype(F32) + cot_rows.astype(F32) * mixed.astype(F32)
    grad_in = grad_in.astype(BF16).reshape(blocks, pos, width)
    return (grad_in, grad_w_in, grad_one, grad_two, grad_kernel)


def solution(mesh):
    fine = Mesh(mesh.devices.reshape(2, 4, 4, 4, 2), ALL)
    return jax.shard_map(
        per_device,
        mesh=fine,
        in_specs=(
            P(CTX, DP, None),
            P(CTX, DP, None),
            P(DP, None),
            P(),
            P(),
            P(CTX, None),
        ),
        out_specs=(P(CTX, DP, None), P(DP, None), P(), P(), P(CTX, None)),
        check_vma=False,
    )
```

```python
import functools
import math

import jax
import jax.numpy as jnp
from jax import lax
from jax.experimental import pallas as pl
from jax.experimental.pallas import tpu as pltpu
from jax.sharding import Mesh
from jax.sharding import PartitionSpec as P

F32 = jnp.float32
BF16 = jnp.bfloat16
ALL = ("zh", "x", "y", "zl", "c")
DP = ("zh", "x")
CTX = ("y", "zl", "c")
LANES = 128
HALF = 64
NN = (((1,), (0,)), ((), ()))
NT = (((1,), (1,)), ((), ()))


def dot(a, b, dims=NN):
    return lax.dot_general(a, b, dims, preferred_element_type=F32)


def call(kernel, outs, scratch, flops, *args, smem=()):
    vmem = pl.BlockSpec(memory_space=pltpu.VMEM)
    specs = [pl.BlockSpec(memory_space=pltpu.SMEM) if i in smem else vmem for i in range(len(args))]
    moved = sum(a.size * a.dtype.itemsize for a in args)
    moved += sum(math.prod(s) * jnp.dtype(t).itemsize for s, t in outs)
    return pl.pallas_call(
        kernel,
        out_shape=[jax.ShapeDtypeStruct(s, t) for s, t in outs],
        in_specs=specs,
        out_specs=[vmem] * len(outs),
        scratch_shapes=scratch,
        compiler_params=pltpu.CompilerParams(vmem_limit_bytes=56 * 2**20),
        cost_estimate=pl.CostEstimate(flops=flops, bytes_accessed=moved, transcendentals=0),
    )(*args)


def widen(lines_ref, buf):
    for r in range(0, buf.shape[0], 512):
        buf[r : r + 512, :] = lines_ref[r : r + 512, :].astype(F32)


def narrow(buf, lines_ref):
    for r in range(0, buf.shape[0], 512):
        lines_ref[r : r + 512, :] = buf[r : r + 512, :].astype(BF16)


def home_store(buf, j, value, count, groups):
    for g in range(groups):
        buf[pl.ds(j * groups + g, value.shape[0], stride=count), :] = value[:, g * LANES : (g + 1) * LANES]


def home_load(buf, j, out_ref, devices, count, groups):
    for g in range(groups):
        value = buf[pl.ds(j * groups + g, devices, stride=count), :]
        out_ref[j * devices : (j + 1) * devices, g * LANES : (g + 1) * LANES] = value.astype(BF16)


def chan_load(buf, j, out_ref, count, groups):
    low = lax.broadcasted_iota(jnp.int32, (32, LANES), 1) < HALF
    for g in range(groups):
        for p in range(4):
            a = buf[pl.ds(2 * p * 32 * count + j * groups + g, 32, stride=count), :]
            b = buf[pl.ds((2 * p + 1) * 32 * count + j * groups + g, 32, stride=count), :]
            even = jnp.where(low, a, pltpu.roll(b, HALF, 1))
            odd = jnp.where(low, pltpu.roll(a, HALF, 1), b)
            lanes = slice(p * LANES, (p + 1) * LANES)
            out_ref[j, 2 * g * 32 : (2 * g + 1) * 32, lanes] = even.astype(BF16)
            out_ref[j, (2 * g + 1) * 32 : (2 * g + 2) * 32, lanes] = odd.astype(BF16)


def chan_store(buf, j, value, count, groups):
    low = lax.broadcasted_iota(jnp.int32, (32, LANES), 1) < HALF
    for g in range(groups):
        for p in range(4):
            lanes = slice(p * LANES, (p + 1) * LANES)
            even = value[2 * g * 32 : (2 * g + 1) * 32, lanes]
            odd = value[(2 * g + 1) * 32 : (2 * g + 2) * 32, lanes]
            a = jnp.where(low, even, pltpu.roll(odd, HALF, 1))
            b = jnp.where(low, pltpu.roll(even, HALF, 1), odd)
            buf[pl.ds(2 * p * 32 * count + j * groups + g, 32, stride=count), :] = a
            buf[pl.ds((2 * p + 1) * 32 * count + j * groups + g, 32, stride=count), :] = b


def unit(size):
    rows = lax.broadcasted_iota(jnp.int32, (size, size), 0)
    cols = lax.broadcasted_iota(jnp.int32, (size, size), 1)
    return jnp.where(rows == cols, 1.0, 0.0).astype(BF16)


def pack_x(count, groups, x_ref, out_ref, buf):
    devices = out_ref.shape[0] // count
    eye = unit(devices)
    for j in range(count // groups):
        turned = dot(eye, x_ref[:, j * devices : (j + 1) * devices], NT)
        home_store(buf, j, turned, count, groups)
    narrow(buf, out_ref)


def pack_h(count, groups, x_ref, cot_ref, w_ref, out_ref, grad_ref, buf):
    devices = out_ref.shape[0] // count
    grad = (cot_ref[...].astype(F32) * x_ref[...].astype(F32)).astype(BF16)
    grad_ref[...] = grad
    for j in range(count // groups):
        value = dot(w_ref[j * devices : (j + 1) * devices, :], grad_ref[...], NT)
        home_store(buf, j, value, count, groups)
    narrow(buf, out_ref)


def forward(count, groups, got_ref, one_ref, two_ref, scale_ref, out_ref, x_ref, y_ref, s_ref, buf, back):
    widen(got_ref, buf)
    for j in range(count // groups):
        chan_load(buf, j, x_ref, count, groups)
        y = dot(x_ref[j], one_ref[...], NT)
        y_ref[j] = y
        s_ref[j] = (scale_ref[...] * y).astype(BF16)
        chan_store(back, j, dot(two_ref[...], s_ref[j]), count, groups)
    narrow(back, out_ref)


def backward(count, groups, got_ref, one_ref, two_ref, scale_ref, y_ref, out_ref, h_ref, t_ref, term_ref, buf, back):
    widen(got_ref, buf)
    for j in range(count // groups):
        chan_load(buf, j, h_ref, count, groups)
        u = dot(two_ref[...], h_ref[j])
        if j == 0:
            term_ref[...] = u * y_ref[j]
        else:
            term_ref[...] += u * y_ref[j]
        t_ref[j] = (scale_ref[...] * u).astype(BF16)
        chan_store(back, j, dot(t_ref[j], one_ref[...]), count, groups)
    narrow(back, out_ref)


def win_parts(count, groups, core_ref, got_ref, grad_ref, mixed_ref, mine_ref, other_ref, buf):
    devices = got_ref.shape[0] // count
    widen(got_ref, buf)
    for j in range(count // groups):
        home_load(buf, j, mixed_ref, devices, count, groups)
    half = mixed_ref.shape[0] // 16
    core = core_ref[0]
    for d in range(8):
        rows = slice(d * half, (d + 1) * half)
        far = pl.multiple_of(d * 2 * half + (1 - core) * half, 32)
        near = pl.multiple_of(d * 2 * half + core * half, 32)
        other_ref[rows, :] = dot(mixed_ref[pl.ds(far, half), :], grad_ref[...]).astype(BF16)
        mine_ref[rows, :] = dot(mixed_ref[pl.ds(near, half), :], grad_ref[...]).astype(BF16)


def mix(mixed_ref, w_ref, out_ref, flat):
    flat[...] = dot(unit(mixed_ref.shape[1]), mixed_ref[...], NT).astype(BF16)
    out_ref[...] = dot(flat[...], w_ref[...]).astype(BF16)


def finish(count, groups, got_ref, cot_ref, mixed_ref, out_ref, buf, turned):
    devices = got_ref.shape[0] // count
    widen(got_ref, buf)
    eye = unit(turned.shape[1])
    for j in range(count // groups):
        home_load(buf, j, turned, devices, count, groups)
        cols = slice(j * devices, (j + 1) * devices)
        back = dot(eye, turned[cols, :], NT)
        gate = cot_ref[:, cols].astype(F32) * mixed_ref[:, cols].astype(F32)
        out_ref[:, cols] = (back + gate).astype(BF16)


def shifted(array, axis, size, step):
    return lax.ppermute(array, axis, [(i, (i + step) % size) for i in range(size)])


def sum_scatter(parts, axis, size):
    me = lax.axis_index(axis)
    total = lax.dynamic_index_in_dim(parts, me, 0, False).astype(F32)
    for step in range(1, size):
        part = lax.dynamic_index_in_dim(parts, (me + step) % size, 0, False)
        total = total + shifted(part, axis, size, step).astype(F32)
    return total


def sum_all(part, axis, size):
    total = part.astype(F32)
    for step in range(1, size):
        total = total + shifted(part, axis, size, step).astype(F32)
    return total


def gather(piece, axis, size):
    me = lax.axis_index(axis)
    pieces = [piece] + [shifted(piece, axis, size, step) for step in range(1, size)]
    held = jnp.stack(pieces)
    return jnp.stack([lax.dynamic_index_in_dim(held, (me - i) % size, 0, False) for i in range(size)])


def gather_w(w_in):
    rows, width = w_in.shape
    piece = rows // 8
    place = lax.axis_index("y") * 2 + lax.axis_index("c")
    mine = lax.dynamic_slice_in_dim(w_in, place * piece, piece, 0)
    other = lax.ppermute(mine, "zh", [(0, 1), (1, 0)])
    low = lax.axis_index("zh") == 0
    both = jnp.concatenate([jnp.where(low, mine, other), jnp.where(low, other, mine)], 0)
    whole = lax.all_gather(both, ("x", "y", "c"), axis=0, tiled=True)
    whole = whole.reshape(4, 8, 2, piece, width).transpose(2, 0, 1, 3, 4)
    return whole.reshape(8 * rows, width)


def exchange(lines):
    return lax.all_to_all(lines, ALL, 0, 0, tiled=True)


def per_device(inputs, cotangent, w_in, factor_one, factor_two, kernel):
    blocks, pos, width = inputs.shape
    tokens = blocks * pos
    devices = 256
    chans = width // devices
    groups = tokens // LANES
    count = chans * groups
    block_len = factor_one.shape[0]
    block_count = factor_two.shape[0]
    lines = (devices * count, LANES)
    buf = pltpu.VMEM(lines, F32)
    shape = (chans, block_count, block_len)
    work = 2 * chans * block_count * block_len
    square = 2 * tokens * width * width

    rows_in = inputs.reshape(tokens, width)
    cot_rows = cotangent.reshape(tokens, width)
    (x_lines,) = call(
        functools.partial(pack_x, count, groups), [(lines, BF16)], [buf], 2 * tokens * width * devices, rows_in
    )
    scale = gather(gather(gather(kernel, "c", 2), "zl", 4), "y", 4)
    scale = scale.reshape(block_count // blocks, blocks, block_len).transpose(1, 0, 2)
    scale = scale.reshape(block_count, block_len)
    two = factor_two.reshape(32, 8, 32, 8).transpose(1, 0, 3, 2).reshape(block_count, block_count)
    whole_w = gather_w(w_in)

    x_got = exchange(x_lines)
    m_lines, xc, yc, sc = call(
        functools.partial(forward, count, groups),
        [(lines, BF16), (shape, BF16), (shape, F32), (shape, BF16)],
        [buf, buf],
        work * (block_len + block_count),
        x_got,
        factor_one,
        two,
        scale,
    )
    m_got = exchange(m_lines)
    h_lines, grad_mixed = call(
        functools.partial(pack_h, count, groups),
        [(lines, BF16), ((tokens, width), BF16)],
        [buf],
        square,
        rows_in,
        cot_rows,
        whole_w,
    )
    h_lines, m_got = lax.optimization_barrier((h_lines, m_got))
    h_got = exchange(h_lines)
    core = lax.axis_index("c")
    mixed_t, mine, other = call(
        functools.partial(win_parts, count, groups),
        [((width, tokens), BF16), ((width // 2, width), BF16), ((width // 2, width), BF16)],
        [buf],
        square,
        core.astype(jnp.int32).reshape(1),
        m_got,
        grad_mixed,
        smem=(0,),
    )
    (mixed,) = call(
        mix, [((tokens, width), BF16)], [pltpu.VMEM((tokens, width), BF16)], square, mixed_t, whole_w
    )
    win = mine.astype(F32) + shifted(other, "c", 2, 1).astype(F32)
    win = win.astype(BF16).reshape(2, 4, 4, -1, width)
    win = sum_scatter(win.transpose(2, 0, 1, 3, 4), "y", 4).astype(BF16)
    win = sum_scatter(win.transpose(1, 0, 2, 3), "x", 4).astype(BF16)
    win = sum_scatter(win, "zh", 2).astype(BF16)
    win = sum_all(win, "zl", 4).astype(BF16)
    win = gather(gather(win, "y", 4), "c", 2).reshape(width // 8, width)
    grad_w_in = win.astype(F32) / math.sqrt(block_count * block_len)

    b_lines, hc, tc, kernel_term = call(
        functools.partial(backward, count, groups),
        [(lines, BF16), (shape, BF16), (shape, BF16), (shape[1:], F32)],
        [buf, buf],
        work * (block_len + block_count),
        h_got,
        factor_one,
        two.T,
        scale,
        yc,
    )
    b_got = exchange(b_lines)
    one_term = jnp.einsum("jap,jaq->pq", tc, xc, preferred_element_type=F32)
    two_term = jnp.einsum("jip,jlp->il", hc, sc, preferred_element_type=F32)
    sizes = (one_term.size // LANES, two_term.size // LANES, kernel_term.size // LANES)
    small = jnp.concatenate([a.reshape(-1, LANES).astype(BF16) for a in (one_term, two_term, kernel_term)], 0)
    small = sum_scatter(small.reshape(2, -1, LANES), "c", 2).astype(BF16)
    small = sum_scatter(small.reshape(4, -1, LANES), "y", 4).astype(BF16)
    small = sum_scatter(small.reshape(4, -1, LANES), "x", 4).astype(BF16)
    small = sum_all(small, "zh", 2).astype(BF16)
    small = sum_all(small, "zl", 4).astype(BF16)
    small = gather(gather(gather(small, "x", 4), "y", 4), "c", 2).reshape(-1, LANES)
    one_total = small[: sizes[0]].astype(F32).reshape(block_len, block_len)
    two_total = small[sizes[0] : sizes[0] + sizes[1]].astype(F32)
    two_total = two_total.reshape(8, 32, 8, 32).transpose(1, 0, 3, 2).reshape(block_count, block_count)
    kernel_total = small[sizes[0] + sizes[1] :].reshape(8, 32, block_len)
    place = (lax.axis_index("y") * 4 + lax.axis_index("zl")) * 2 + core
    kernel_total = lax.dynamic_index_in_dim(kernel_total, place, 1, False).astype(F32)
    grad_kernel = kernel_total / math.sqrt(width)
    grad_one = one_total / math.sqrt(block_count * width)
    grad_two = two_total / math.sqrt(block_len * width)

    (grad_in,) = call(
        functools.partial(finish, count, groups),
        [((tokens, width), BF16)],
        [buf, pltpu.VMEM((width, tokens), BF16)],
        2 * tokens * tokens * width,
        b_got,
        cot_rows,
        mixed,
    )
    return (grad_in.reshape(inputs.shape), grad_w_in, grad_one, grad_two, grad_kernel)


def solution(mesh):
    fine = Mesh(mesh.devices.reshape(2, 4, 4, 4, 2), ALL)
    return jax.shard_map(
        per_device,
        mesh=fine,
        in_specs=(
            P(CTX, DP, None),
            P(CTX, DP, None),
            P(DP, None),
            P(),
            P(),
            P(CTX, None),
        ),
        out_specs=(P(CTX, DP, None), P(DP, None), P(), P(), P(CTX, None)),
        check_vma=False,
    )
```

```python
import functools
import math

import jax
import jax.numpy as jnp
from jax import lax
from jax.experimental import pallas as pl
from jax.experimental.pallas import tpu as pltpu
from jax.sharding import Mesh
from jax.sharding import PartitionSpec as P

F32 = jnp.float32
BF16 = jnp.bfloat16
ALL = ("zh", "x", "y", "zl", "c")
DP = ("zh", "x")
CTX = ("y", "zl", "c")
LANES = 128
HALF = 64
NN = (((1,), (0,)), ((), ()))
NT = (((1,), (1,)), ((), ()))
TN = (((0,), (0,)), ((), ()))


def dot(a, b, dims=NN):
    return lax.dot_general(a, b, dims, preferred_element_type=F32)


def call(kernel, outs, scratch, *args, smem=()):
    vmem = pl.BlockSpec(memory_space=pltpu.VMEM)
    specs = [pl.BlockSpec(memory_space=pltpu.SMEM) if i in smem else vmem for i in range(len(args))]
    return pl.pallas_call(
        kernel,
        out_shape=[jax.ShapeDtypeStruct(s, t) for s, t in outs],
        in_specs=specs,
        out_specs=[vmem] * len(outs),
        scratch_shapes=scratch,
        compiler_params=pltpu.CompilerParams(vmem_limit_bytes=56 * 2**20),
        cost_estimate=pl.CostEstimate(flops=1000, bytes_accessed=1000, transcendentals=0),
    )(*args)


def widen(lines_ref, buf):
    for r in range(0, buf.shape[0], 512):
        buf[r : r + 512, :] = lines_ref[r : r + 512, :].astype(F32)


def narrow(buf, lines_ref):
    for r in range(0, buf.shape[0], 512):
        lines_ref[r : r + 512, :] = buf[r : r + 512, :].astype(BF16)


def home_store(buf, j, value, count, groups):
    for g in range(groups):
        buf[pl.ds(j * groups + g, value.shape[0], stride=count), :] = value[:, g * LANES : (g + 1) * LANES]


def home_load(buf, j, out_ref, devices, count, groups):
    for g in range(groups):
        value = buf[pl.ds(j * groups + g, devices, stride=count), :]
        out_ref[j * devices : (j + 1) * devices, g * LANES : (g + 1) * LANES] = value.astype(BF16)


def chan_load(buf, j, out_ref, count, groups):
    low = lax.broadcasted_iota(jnp.int32, (32, LANES), 1) < HALF
    for g in range(groups):
        for p in range(4):
            a = buf[pl.ds(2 * p * 32 * count + j * groups + g, 32, stride=count), :]
            b = buf[pl.ds((2 * p + 1) * 32 * count + j * groups + g, 32, stride=count), :]
            even = jnp.where(low, a, pltpu.roll(b, HALF, 1))
            odd = jnp.where(low, pltpu.roll(a, HALF, 1), b)
            lanes = slice(p * LANES, (p + 1) * LANES)
            out_ref[j, 2 * g * 32 : (2 * g + 1) * 32, lanes] = even.astype(BF16)
            out_ref[j, (2 * g + 1) * 32 : (2 * g + 2) * 32, lanes] = odd.astype(BF16)


def chan_store(buf, j, value, count, groups):
    low = lax.broadcasted_iota(jnp.int32, (32, LANES), 1) < HALF
    for g in range(groups):
        for p in range(4):
            lanes = slice(p * LANES, (p + 1) * LANES)
            even = value[2 * g * 32 : (2 * g + 1) * 32, lanes]
            odd = value[(2 * g + 1) * 32 : (2 * g + 2) * 32, lanes]
            a = jnp.where(low, even, pltpu.roll(odd, HALF, 1))
            b = jnp.where(low, pltpu.roll(even, HALF, 1), odd)
            buf[pl.ds(2 * p * 32 * count + j * groups + g, 32, stride=count), :] = a
            buf[pl.ds((2 * p + 1) * 32 * count + j * groups + g, 32, stride=count), :] = b


def unit(size):
    rows = lax.broadcasted_iota(jnp.int32, (size, size), 0)
    cols = lax.broadcasted_iota(jnp.int32, (size, size), 1)
    return jnp.where(rows == cols, 1.0, 0.0).astype(BF16)


def pack_x(count, groups, x_ref, out_ref, buf):
    devices = out_ref.shape[0] // count
    eye = unit(devices)
    for j in range(count // groups):
        turned = dot(eye, x_ref[:, j * devices : (j + 1) * devices], NT)
        home_store(buf, j, turned, count, groups)
    narrow(buf, out_ref)


def pack_h(count, groups, x_ref, cot_ref, w_ref, out_ref, grad_ref, buf):
    devices = out_ref.shape[0] // count
    grad = (cot_ref[...].astype(F32) * x_ref[...].astype(F32)).astype(BF16)
    grad_ref[...] = grad
    for j in range(count // groups):
        value = dot(w_ref[j * devices : (j + 1) * devices, :], grad_ref[...], NT)
        home_store(buf, j, value, count, groups)
    narrow(buf, out_ref)


def forward(count, groups, got_ref, one_ref, two_ref, scale_ref, out_ref, x_ref, s_ref, buf, back):
    widen(got_ref, buf)
    for j in range(count // groups):
        chan_load(buf, j, x_ref, count, groups)
        s_ref[j] = (scale_ref[...] * dot(x_ref[j], one_ref[...], NT)).astype(BF16)
        chan_store(back, j, dot(two_ref[...], s_ref[j]), count, groups)
    narrow(back, out_ref)


def backward(count, groups, got_ref, one_ref, two_ref, scale_ref, out_ref, h_ref, t_ref, buf, back):
    widen(got_ref, buf)
    for j in range(count // groups):
        chan_load(buf, j, h_ref, count, groups)
        t_ref[j] = (scale_ref[...] * dot(two_ref[...], h_ref[j])).astype(BF16)
        chan_store(back, j, dot(t_ref[j], one_ref[...]), count, groups)
    narrow(back, out_ref)


def factor_sums(weights, one_ref, two_ref, x_ref, s_ref, h_ref, t_ref, out_ref, tall, term):
    chans, count, length = x_ref.shape
    square = jnp.zeros((count, count), F32)
    for j in range(chans):
        part = dot(two_ref[...], h_ref[j]) * dot(x_ref[j], one_ref[...], NT)
        term[...] = part if j == 0 else term[...] + part
        square += dot(h_ref[j], s_ref[j], NT)
        part = lax.dot_general(t_ref[j], x_ref[j], TN, preferred_element_type=F32)
        tall[...] = part if j == 0 else tall[...] + part
    out_ref[:length, :] = (tall[...] * weights[0]).astype(BF16)
    out_ref[length : length + count, :] = (term[...] * weights[1]).astype(BF16)
    rows = lax.broadcasted_iota(jnp.int32, (count, count), 0)
    cols = lax.broadcasted_iota(jnp.int32, (count, count), 1)
    turn = jnp.where(cols == lax.rem(rows, 8) * 32 + lax.div(rows, 8), 1.0, 0.0).astype(BF16)
    square = dot(turn, (square * weights[2]).astype(BF16)).astype(BF16)
    out_ref[length + count :, :count] = dot(square, turn, NT).astype(BF16)
    out_ref[length + count :, count:] = jnp.zeros((count, length - count), BF16)


def open_mixed(count, groups, core_ref, got_ref, mixed_ref, near_ref, far_ref, buf):
    devices = got_ref.shape[0] // count
    widen(got_ref, buf)
    for j in range(count // groups):
        home_load(buf, j, mixed_ref, devices, count, groups)
    half = mixed_ref.shape[0] // 16
    core = core_ref[0]
    for d in range(8):
        rows = slice(d * half, (d + 1) * half)
        near = pl.multiple_of(d * 2 * half + core * half, 32)
        far = pl.multiple_of(d * 2 * half + (1 - core) * half, 32)
        near_ref[rows, :] = mixed_ref[pl.ds(near, half), :]
        far_ref[rows, :] = mixed_ref[pl.ds(far, half), :]


def win_parts(near_ref, grad_ref, far_ref, far_grad_ref, by_y_ref, by_x_ref):
    rows, cols = by_y_ref.shape[3:]
    for y in range(4):
        lanes = slice(y * cols, (y + 1) * cols)
        part = dot(near_ref[...], grad_ref[:, lanes]) + dot(far_ref[...], far_grad_ref[:, lanes])
        part = part.astype(BF16)
        for d in range(8):
            first = 2 * d * rows
            by_y_ref[y, d // 4, d % 4] = part[first : first + rows, :]
            by_x_ref[d % 4, d // 4, y] = part[first + rows : first + 2 * rows, :]


def mix(mixed_ref, w_ref, out_ref, flat):
    flat[...] = dot(unit(mixed_ref.shape[1]), mixed_ref[...], NT).astype(BF16)
    out_ref[...] = dot(flat[...], w_ref[...]).astype(BF16)


def finish(count, groups, got_ref, cot_ref, mixed_ref, out_ref, buf, turned):
    devices = got_ref.shape[0] // count
    widen(got_ref, buf)
    eye = unit(turned.shape[1])
    for j in range(count // groups):
        home_load(buf, j, turned, devices, count, groups)
        cols = slice(j * devices, (j + 1) * devices)
        back = dot(eye, turned[cols, :], NT)
        gate = cot_ref[:, cols].astype(F32) * mixed_ref[:, cols].astype(F32)
        out_ref[:, cols] = (back + gate).astype(BF16)


def shifted(array, axis, size, step):
    return lax.ppermute(array, axis, [(i, (i + step) % size) for i in range(size)])


def sum_scatter(parts, axis, size, dim=0, own=None):
    me = lax.axis_index(axis)
    total = lax.dynamic_index_in_dim(parts, me, dim, False) if own is None else own
    total = total.astype(F32)
    for step in range(1, size):
        part = lax.dynamic_index_in_dim(parts, (me + step) % size, dim, False).astype(BF16)
        total = total + shifted(part, axis, size, step).astype(F32)
    return total


def sum_all(part, axis, size):
    total = part
    for step in range(1, size):
        total = total + shifted(part.astype(BF16), axis, size, step).astype(F32)
    return total


def gather(piece, axis, size, dim=None):
    me = lax.axis_index(axis)
    pieces = [piece] + [shifted(piece, axis, size, step) for step in range(1, size)]
    placed = [lax.select_n((me - i) % size, *pieces) if size > 2 else jnp.where(me == i, *pieces) for i in range(size)]
    return jnp.stack(placed) if dim is None else jnp.concatenate(placed, dim)


def w_piece(w_in):
    piece = w_in.shape[0] // 8
    place = lax.axis_index("y") * 2 + lax.axis_index("c")
    mine = lax.dynamic_slice_in_dim(w_in, place * piece, piece, 0)
    return mine, lax.ppermute(mine, "zh", [(0, 1), (1, 0)])


def gather_w(mine, other):
    piece, width = mine.shape
    low = lax.axis_index("zh") == 0
    both = jnp.concatenate([jnp.where(low, mine, other), jnp.where(low, other, mine)], 0)
    whole = lax.all_gather(both, ("x", "y", "c"), axis=0, tiled=True)
    whole = whole.reshape(4, 8, 2, piece, width).transpose(2, 0, 1, 3, 4)
    return whole.reshape(64 * piece, width)


def tied(*arrays):
    return lax.optimization_barrier(arrays)


def exchange(lines):
    return lax.all_to_all(lines, ALL, 0, 0, tiled=True)


def per_device(inputs, cotangent, w_in, factor_one, factor_two, kernel):
    blocks, pos, width = inputs.shape
    tokens = blocks * pos
    devices = 256
    chans = width // devices
    groups = tokens // LANES
    count = chans * groups
    block_len = factor_one.shape[0]
    block_count = factor_two.shape[0]
    lines = (devices * count, LANES)
    buf = pltpu.VMEM(lines, F32)
    shape = (chans, block_count, block_len)

    rows_in = inputs.reshape(tokens, width)
    cot_rows = cotangent.reshape(tokens, width)
    core = lax.axis_index("c")
    scale = gather(kernel, "zl", 4)
    w_mine, w_other = w_piece(w_in)
    (x_lines,) = call(functools.partial(pack_x, count, groups), [(lines, BF16)], [buf], rows_in)
    x_lines, scale, w_other = tied(x_lines, scale, w_other)
    x_got = exchange(x_lines)
    scale = gather(gather(scale, "y", 4), "c", 2)
    scale = scale.transpose(3, 1, 2, 0, 4).reshape(block_count, block_len)
    two = factor_two.reshape(32, 8, 32, 8).transpose(1, 0, 3, 2).reshape(block_count, block_count)
    whole_w = gather_w(w_mine, w_other)

    m_lines, xc, sc = call(
        functools.partial(forward, count, groups),
        [(lines, BF16), (shape, BF16), (shape, BF16)],
        [buf, buf],
        x_got,
        factor_one,
        two,
        scale,
    )
    m_got = exchange(m_lines)
    h_lines, grad_mixed = call(
        functools.partial(pack_h, count, groups),
        [(lines, BF16), ((tokens, width), BF16)],
        [buf],
        rows_in,
        cot_rows,
        whole_w,
    )
    far_grad = shifted(grad_mixed, "c", 2, 1)
    h_lines, m_got = tied(h_lines, m_got)
    h_got = exchange(h_lines)
    mixed_t, near, far = call(
        functools.partial(open_mixed, count, groups),
        [((width, tokens), BF16), ((width // 2, tokens), BF16), ((width // 2, tokens), BF16)],
        [buf],
        core.astype(jnp.int32).reshape(1),
        m_got,
        smem=(0,),
    )
    far = shifted(far, "c", 2, 1)
    cols = width // 4
    part = (4, 2, 4, width // 32, cols)
    win_y, win_x = call(win_parts, [(part, BF16), (part, BF16)], [], near, grad_mixed, far, far_grad)
    win_y = sum_scatter(win_y, "y", 4)
    win_x = sum_scatter(win_x, "x", 4)
    h_got, win_y, win_x = tied(h_got, win_y, win_x)
    win_y = win_y.transpose(1, 0, 2, 3).reshape(-1, cols)
    win_y = lax.psum_scatter(win_y, "x", scatter_dimension=0, tiled=True).reshape(2, -1, cols)

    b_lines, hc, tc = call(
        functools.partial(backward, count, groups),
        [(lines, BF16), (shape, BF16), (shape, BF16)],
        [buf, buf],
        h_got,
        factor_one,
        two.T,
        scale,
    )
    b_got = exchange(b_lines)
    weights = [1 / math.sqrt(n) for n in (block_count * width, width, block_len * width)]
    (small,) = call(
        functools.partial(factor_sums, weights),
        [((block_len + 2 * block_count, block_len), BF16)],
        [pltpu.VMEM((block_len, block_len), F32), pltpu.VMEM((block_count, block_len), F32)],
        factor_one,
        two.T,
        xc,
        sc,
        hc,
        tc,
    )
    small = sum_scatter(small.reshape(2, -1, block_len), "c", 2)
    small = sum_scatter(small.reshape(4, -1, block_len), "y", 4)
    small = sum_scatter(small.reshape(4, -1, block_len), "x", 4)
    win_x = sum_scatter(win_x, "y", 4, 1)
    small, b_got, win_y, win_x = tied(small, b_got, win_y, win_x)
    win = jnp.concatenate([win_y, win_x], 1)
    win = win.reshape(2, -1, block_len)
    z_half = lax.axis_index("zh")
    mine = jnp.concatenate([lax.dynamic_index_in_dim(win, z_half, 0, False), small], 0)
    other = jnp.concatenate([lax.dynamic_index_in_dim(win, 1 - z_half, 0, False), small], 0)
    both = mine + shifted(other.astype(BF16), "zh", 2, 1).astype(F32)
    both = sum_all(both, "zl", 4)
    small = both[win.shape[1] :].astype(BF16)
    win = both[: win.shape[1]].reshape(-1, cols) / math.sqrt(block_count * block_len)
    small = jnp.broadcast_to(small[None], (32,) + small.shape).reshape(-1, block_len)
    small = lax.all_to_all(small, ("x", "y", "c"), 0, 0, tiled=True).reshape(4, 4, 2, -1, block_len)
    small = small.transpose(2, 1, 0, 3, 4).reshape(-1, block_len).astype(F32)
    win = lax.all_gather(win, ("y", "c"), axis=0).reshape(4, 2, -1, cols)
    grad_w_in = win.transpose(1, 2, 0, 3).reshape(width // 8, width)
    grad_one = small[:block_len]
    kernel_total = small[block_len : block_len + block_count].reshape(8, 32, block_len)
    place = (lax.axis_index("y") * 4 + lax.axis_index("zl")) * 2 + core
    grad_kernel = lax.dynamic_index_in_dim(kernel_total, place, 1, False)
    grad_two = small[block_len + block_count :, :block_count]

    (mixed,) = call(mix, [((tokens, width), BF16)], [pltpu.VMEM((tokens, width), BF16)], mixed_t, whole_w)
    (grad_in,) = call(
        functools.partial(finish, count, groups),
        [((tokens, width), BF16)],
        [buf, pltpu.VMEM((width, tokens), BF16)],
        b_got,
        cot_rows,
        mixed,
    )
    return (grad_in.reshape(inputs.shape), grad_w_in, grad_one, grad_two, grad_kernel)


def solution(mesh):
    fine = Mesh(mesh.devices.reshape(2, 4, 4, 4, 2), ALL)
    return jax.shard_map(
        per_device,
        mesh=fine,
        in_specs=(
            P(CTX, DP, None),
            P(CTX, DP, None),
            P(DP, None),
            P(),
            P(),
            P(CTX, None),
        ),
        out_specs=(P(CTX, DP, None), P(DP, None), P(), P(), P(CTX, None)),
        check_vma=False,
    )
```

```python
import functools
import math

import jax
import jax.numpy as jnp
from jax import lax
from jax.experimental import pallas as pl
from jax.experimental.pallas import tpu as pltpu
from jax.sharding import Mesh
from jax.sharding import PartitionSpec as P

F32 = jnp.float32
BF16 = jnp.bfloat16
ALL = ("zh", "x", "y", "zl", "c")
DP = ("zh", "x")
CTX = ("y", "zl", "c")
LANES = 128
HALF = 64
NN = (((1,), (0,)), ((), ()))
NT = (((1,), (1,)), ((), ()))
TN = (((0,), (0,)), ((), ()))


def dot(a, b, dims=NN):
    return lax.dot_general(a, b, dims, preferred_element_type=F32)


def call(kernel, outs, scratch, *args, smem=()):
    vmem = pl.BlockSpec(memory_space=pltpu.VMEM)
    specs = [pl.BlockSpec(memory_space=pltpu.SMEM) if i in smem else vmem for i in range(len(args))]
    return pl.pallas_call(
        kernel,
        out_shape=[jax.ShapeDtypeStruct(s, t) for s, t in outs],
        in_specs=specs,
        out_specs=[vmem] * len(outs),
        scratch_shapes=scratch,
        compiler_params=pltpu.CompilerParams(vmem_limit_bytes=56 * 2**20),
        cost_estimate=pl.CostEstimate(flops=1000, bytes_accessed=1000, transcendentals=0),
    )(*args)


def widen(lines_ref, buf):
    for r in range(0, buf.shape[0], 512):
        buf[r : r + 512, :] = lines_ref[r : r + 512, :].astype(F32)


def narrow(buf, lines_ref):
    for r in range(0, buf.shape[0], 512):
        lines_ref[r : r + 512, :] = buf[r : r + 512, :].astype(BF16)


def home_store(buf, j, value, count, groups):
    for g in range(groups):
        buf[pl.ds(j * groups + g, value.shape[0], stride=count), :] = value[:, g * LANES : (g + 1) * LANES]


def home_load(buf, j, out_ref, devices, count, groups):
    for g in range(groups):
        value = buf[pl.ds(j * groups + g, devices, stride=count), :]
        out_ref[j * devices : (j + 1) * devices, g * LANES : (g + 1) * LANES] = value.astype(BF16)


def chan_load(buf, j, out_ref, count, groups):
    low = lax.broadcasted_iota(jnp.int32, (32, LANES), 1) < HALF
    for g in range(groups):
        for p in range(4):
            a = buf[pl.ds(2 * p * 32 * count + j * groups + g, 32, stride=count), :]
            b = buf[pl.ds((2 * p + 1) * 32 * count + j * groups + g, 32, stride=count), :]
            even = jnp.where(low, a, pltpu.roll(b, HALF, 1))
            odd = jnp.where(low, pltpu.roll(a, HALF, 1), b)
            lanes = slice(p * LANES, (p + 1) * LANES)
            out_ref[j, 2 * g * 32 : (2 * g + 1) * 32, lanes] = even.astype(BF16)
            out_ref[j, (2 * g + 1) * 32 : (2 * g + 2) * 32, lanes] = odd.astype(BF16)


def chan_store(buf, j, value, count, groups):
    low = lax.broadcasted_iota(jnp.int32, (32, LANES), 1) < HALF
    for g in range(groups):
        for p in range(4):
            lanes = slice(p * LANES, (p + 1) * LANES)
            even = value[2 * g * 32 : (2 * g + 1) * 32, lanes]
            odd = value[(2 * g + 1) * 32 : (2 * g + 2) * 32, lanes]
            a = jnp.where(low, even, pltpu.roll(odd, HALF, 1))
            b = jnp.where(low, pltpu.roll(even, HALF, 1), odd)
            buf[pl.ds(2 * p * 32 * count + j * groups + g, 32, stride=count), :] = a
            buf[pl.ds((2 * p + 1) * 32 * count + j * groups + g, 32, stride=count), :] = b


def unit(size):
    rows = lax.broadcasted_iota(jnp.int32, (size, size), 0)
    cols = lax.broadcasted_iota(jnp.int32, (size, size), 1)
    return jnp.where(rows == cols, 1.0, 0.0).astype(BF16)


def pack_x(count, groups, x_ref, out_ref, buf):
    devices = out_ref.shape[0] // count
    eye = unit(devices)
    for j in range(count // groups):
        turned = dot(eye, x_ref[:, j * devices : (j + 1) * devices], NT)
        home_store(buf, j, turned, count, groups)
    narrow(buf, out_ref)


def pack_h(count, groups, x_ref, cot_ref, w_ref, out_ref, grad_ref, buf):
    devices = out_ref.shape[0] // count
    grad = (cot_ref[...].astype(F32) * x_ref[...].astype(F32)).astype(BF16)
    grad_ref[...] = grad
    for j in range(count // groups):
        value = dot(w_ref[j * devices : (j + 1) * devices, :], grad_ref[...], NT)
        home_store(buf, j, value, count, groups)
    narrow(buf, out_ref)


def forward(count, groups, got_ref, one_ref, two_ref, scale_ref, out_ref, x_ref, s_ref, buf, back):
    widen(got_ref, buf)
    for j in range(count // groups):
        chan_load(buf, j, x_ref, count, groups)
        s_ref[j] = (scale_ref[...] * dot(x_ref[j], one_ref[...], NT)).astype(BF16)
        chan_store(back, j, dot(two_ref[...], s_ref[j]), count, groups)
    narrow(back, out_ref)


def backward(count, groups, got_ref, one_ref, two_ref, scale_ref, out_ref, h_ref, t_ref, buf, back):
    widen(got_ref, buf)
    for j in range(count // groups):
        chan_load(buf, j, h_ref, count, groups)
        t_ref[j] = (scale_ref[...] * dot(two_ref[...], h_ref[j])).astype(BF16)
        chan_store(back, j, dot(t_ref[j], one_ref[...]), count, groups)
    narrow(back, out_ref)


def factor_sums(weights, one_ref, two_ref, x_ref, s_ref, h_ref, t_ref, out_ref, tall, term):
    chans, count, length = x_ref.shape
    square = jnp.zeros((count, count), F32)
    for j in range(chans):
        part = dot(two_ref[...], h_ref[j]) * dot(x_ref[j], one_ref[...], NT)
        term[...] = part if j == 0 else term[...] + part
        square += dot(h_ref[j], s_ref[j], NT)
        part = lax.dot_general(t_ref[j], x_ref[j], TN, preferred_element_type=F32)
        tall[...] = part if j == 0 else tall[...] + part
    out_ref[:length, :] = (tall[...] * weights[0]).astype(BF16)
    out_ref[length : length + count, :] = (term[...] * weights[1]).astype(BF16)
    rows = lax.broadcasted_iota(jnp.int32, (count, count), 0)
    cols = lax.broadcasted_iota(jnp.int32, (count, count), 1)
    turn = jnp.where(cols == lax.rem(rows, 8) * 32 + lax.div(rows, 8), 1.0, 0.0).astype(BF16)
    square = dot(turn, (square * weights[2]).astype(BF16)).astype(BF16)
    out_ref[length + count :, :count] = dot(square, turn, NT).astype(BF16)
    out_ref[length + count :, count:] = jnp.zeros((count, length - count), BF16)


def open_mixed(count, groups, core_ref, got_ref, mixed_ref, near_ref, far_ref, buf):
    devices = got_ref.shape[0] // count
    widen(got_ref, buf)
    for j in range(count // groups):
        home_load(buf, j, mixed_ref, devices, count, groups)
    half = mixed_ref.shape[0] // 32
    core = core_ref[0]
    for d in range(8):
        rows = slice(d * half, (d + 1) * half)
        for part in range(2):
            near = pl.multiple_of((4 * d + part) * half + 2 * core * half, 16)
            far = pl.multiple_of((4 * d + part) * half + 2 * (1 - core) * half, 16)
            near_ref[part, rows, :] = mixed_ref[pl.ds(near, half), :]
            far_ref[part, rows, :] = mixed_ref[pl.ds(far, half), :]


def win_parts(by_rows, near_ref, grad_ref, far_ref, far_grad_ref, out_ref):
    rows, cols = out_ref.shape[3:]
    for y in range(4):
        lanes = slice(y * cols, (y + 1) * cols)
        part = dot(near_ref[by_rows], grad_ref[:, lanes]) + dot(far_ref[by_rows], far_grad_ref[:, lanes])
        part = part.astype(BF16)
        for d in range(8):
            place = (d % 4, d // 4, y) if by_rows else (y, d // 4, d % 4)
            out_ref[place] = part[d * rows : (d + 1) * rows, :]


def mix(mixed_ref, w_ref, out_ref, flat):
    flat[...] = dot(unit(mixed_ref.shape[1]), mixed_ref[...], NT).astype(BF16)
    out_ref[...] = dot(flat[...], w_ref[...]).astype(BF16)


def finish(count, groups, got_ref, cot_ref, mixed_ref, out_ref, buf, turned):
    devices = got_ref.shape[0] // count
    widen(got_ref, buf)
    eye = unit(turned.shape[1])
    for j in range(count // groups):
        home_load(buf, j, turned, devices, count, groups)
        cols = slice(j * devices, (j + 1) * devices)
        back = dot(eye, turned[cols, :], NT)
        gate = cot_ref[:, cols].astype(F32) * mixed_ref[:, cols].astype(F32)
        out_ref[:, cols] = (back + gate).astype(BF16)


def shifted(array, axis, size, step):
    return lax.ppermute(array, axis, [(i, (i + step) % size) for i in range(size)])


def sum_scatter(parts, axis, size, dim=0, own=None):
    me = lax.axis_index(axis)
    total = lax.dynamic_index_in_dim(parts, me, dim, False) if own is None else own
    total = total.astype(F32)
    for step in range(1, size):
        part = lax.dynamic_index_in_dim(parts, (me + step) % size, dim, False).astype(BF16)
        total = total + shifted(part, axis, size, step).astype(F32)
    return total


def sum_all(part, axis, size):
    total = part
    for step in range(1, size):
        total = total + shifted(part.astype(BF16), axis, size, step).astype(F32)
    return total


def gather(piece, axis, size, dim=None):
    me = lax.axis_index(axis)
    pieces = [piece] + [shifted(piece, axis, size, step) for step in range(1, size)]
    placed = [lax.select_n((me - i) % size, *pieces) if size > 2 else jnp.where(me == i, *pieces) for i in range(size)]
    return jnp.stack(placed) if dim is None else jnp.concatenate(placed, dim)


def w_piece(w_in):
    piece = w_in.shape[0] // 8
    place = lax.axis_index("y") * 2 + lax.axis_index("c")
    mine = lax.dynamic_slice_in_dim(w_in, place * piece, piece, 0)
    return mine, lax.ppermute(mine, "zh", [(0, 1), (1, 0)])


def gather_w(mine, other):
    piece, width = mine.shape
    low = lax.axis_index("zh") == 0
    both = jnp.concatenate([jnp.where(low, mine, other), jnp.where(low, other, mine)], 0)
    whole = lax.all_gather(both, ("x", "y", "c"), axis=0, tiled=True)
    whole = whole.reshape(4, 8, 2, piece, width).transpose(2, 0, 1, 3, 4)
    return whole.reshape(64 * piece, width)


def tied(*arrays):
    return lax.optimization_barrier(arrays)


def exchange(lines):
    return lax.all_to_all(lines, ALL, 0, 0, tiled=True)


def per_device(inputs, cotangent, w_in, factor_one, factor_two, kernel):
    blocks, pos, width = inputs.shape
    tokens = blocks * pos
    devices = 256
    chans = width // devices
    groups = tokens // LANES
    count = chans * groups
    block_len = factor_one.shape[0]
    block_count = factor_two.shape[0]
    lines = (devices * count, LANES)
    buf = pltpu.VMEM(lines, F32)
    shape = (chans, block_count, block_len)

    rows_in = inputs.reshape(tokens, width)
    cot_rows = cotangent.reshape(tokens, width)
    core = lax.axis_index("c")
    scale = gather(kernel, "zl", 4)
    w_mine, w_other = w_piece(w_in)
    (x_lines,) = call(functools.partial(pack_x, count, groups), [(lines, BF16)], [buf], rows_in)
    x_lines, scale, w_other = tied(x_lines, scale, w_other)
    x_got = exchange(x_lines)
    scale = gather(gather(scale, "y", 4), "c", 2)
    scale = scale.transpose(3, 1, 2, 0, 4).reshape(block_count, block_len)
    two = factor_two.reshape(32, 8, 32, 8).transpose(1, 0, 3, 2).reshape(block_count, block_count)
    whole_w = gather_w(w_mine, w_other)

    m_lines, xc, sc = call(
        functools.partial(forward, count, groups),
        [(lines, BF16), (shape, BF16), (shape, BF16)],
        [buf, buf],
        x_got,
        factor_one,
        two,
        scale,
    )
    m_got = exchange(m_lines)
    h_lines, grad_mixed = call(
        functools.partial(pack_h, count, groups),
        [(lines, BF16), ((tokens, width), BF16)],
        [buf],
        rows_in,
        cot_rows,
        whole_w,
    )
    far_grad = shifted(grad_mixed, "c", 2, 1)
    h_lines, m_got = tied(h_lines, m_got)
    h_got = exchange(h_lines)
    mixed_t, near, far = call(
        functools.partial(open_mixed, count, groups),
        [((width, tokens), BF16), ((2, width // 4, tokens), BF16), ((2, width // 4, tokens), BF16)],
        [buf],
        core.astype(jnp.int32).reshape(1),
        m_got,
        smem=(0,),
    )
    far = shifted(far, "c", 2, 1)
    cols = width // 4
    part = (4, 2, 4, width // 32, cols)
    (win_y,) = call(functools.partial(win_parts, 0), [(part, BF16)], [], near, grad_mixed, far, far_grad)
    (win_x,) = call(functools.partial(win_parts, 1), [(part, BF16)], [], near, grad_mixed, far, far_grad)
    win_y = sum_scatter(win_y, "y", 4)
    win_x = sum_scatter(win_x, "x", 4)
    h_got, win_y, win_x = tied(h_got, win_y, win_x)
    win_y = win_y.transpose(1, 0, 2, 3).reshape(-1, cols)
    win_y = lax.psum_scatter(win_y, "x", scatter_dimension=0, tiled=True).reshape(2, -1, cols)

    b_lines, hc, tc = call(
        functools.partial(backward, count, groups),
        [(lines, BF16), (shape, BF16), (shape, BF16)],
        [buf, buf],
        h_got,
        factor_one,
        two.T,
        scale,
    )
    b_got = exchange(b_lines)
    weights = [1 / math.sqrt(n) for n in (block_count * width, width, block_len * width)]
    (small,) = call(
        functools.partial(factor_sums, weights),
        [((block_len + 2 * block_count, block_len), BF16)],
        [pltpu.VMEM((block_len, block_len), F32), pltpu.VMEM((block_count, block_len), F32)],
        factor_one,
        two.T,
        xc,
        sc,
        hc,
        tc,
    )
    small = sum_scatter(small.reshape(2, -1, block_len), "c", 2)
    small = sum_scatter(small.reshape(4, -1, block_len), "y", 4)
    small = sum_scatter(small.reshape(4, -1, block_len), "x", 4)
    win_x = sum_scatter(win_x, "y", 4, 1)
    small, b_got, win_y, win_x = tied(small, b_got, win_y, win_x)
    win = jnp.concatenate([win_y, win_x], 1)
    win = win.reshape(2, -1, block_len)
    z_half = lax.axis_index("zh")
    mine = jnp.concatenate([lax.dynamic_index_in_dim(win, z_half, 0, False), small], 0)
    other = jnp.concatenate([lax.dynamic_index_in_dim(win, 1 - z_half, 0, False), small], 0)
    both = mine + shifted(other.astype(BF16), "zh", 2, 1).astype(F32)
    both = sum_all(both, "zl", 4)
    small = both[win.shape[1] :].astype(BF16)
    win = both[: win.shape[1]].reshape(-1, cols) / math.sqrt(block_count * block_len)
    small = jnp.broadcast_to(small[None], (32,) + small.shape).reshape(-1, block_len)
    small = lax.all_to_all(small, ("x", "y", "c"), 0, 0, tiled=True).reshape(4, 4, 2, -1, block_len)
    small = small.transpose(2, 1, 0, 3, 4).reshape(-1, block_len).astype(F32)
    win = lax.all_gather(win, ("y", "c"), axis=0).reshape(4, 2, -1, cols)
    grad_w_in = win.transpose(1, 2, 0, 3).reshape(width // 8, width)
    grad_one = small[:block_len]
    kernel_total = small[block_len : block_len + block_count].reshape(8, 32, block_len)
    place = (lax.axis_index("y") * 4 + lax.axis_index("zl")) * 2 + core
    grad_kernel = lax.dynamic_index_in_dim(kernel_total, place, 1, False)
    grad_two = small[block_len + block_count :, :block_count]

    (mixed,) = call(mix, [((tokens, width), BF16)], [pltpu.VMEM((tokens, width), BF16)], mixed_t, whole_w)
    (grad_in,) = call(
        functools.partial(finish, count, groups),
        [((tokens, width), BF16)],
        [buf, pltpu.VMEM((width, tokens), BF16)],
        b_got,
        cot_rows,
        mixed,
    )
    return (grad_in.reshape(inputs.shape), grad_w_in, grad_one, grad_two, grad_kernel)


def solution(mesh):
    fine = Mesh(mesh.devices.reshape(2, 4, 4, 4, 2), ALL)
    return jax.shard_map(
        per_device,
        mesh=fine,
        in_specs=(
            P(CTX, DP, None),
            P(CTX, DP, None),
            P(DP, None),
            P(),
            P(),
            P(CTX, None),
        ),
        out_specs=(P(CTX, DP, None), P(DP, None), P(), P(), P(CTX, None)),
        check_vma=False,
    )
```
